512 devices in a mesh: dp: 128 (over y, z, core), group: 4 (over x).
Axes of the slice: x: 4, y: 8, z: 8, core: 2. Of those that a mesh axis runs over, the one named last changes fastest.
Arguments:
- gradient: float32 [176, 1024, 768], P(None, ('dp', 'group')), may hold values from -90 to 90
- momentum: float32 [176, 1024, 768], P(None, ('dp', 'group')), may hold values from -90 to 90
- weight: bfloat16 [176, 1024, 768], P(None, ('dp', 'group')), may hold values from -0.21875 to 0.21875
Outputs:
- new_momentum: float32 [176, 1024, 768], P(None, ('dp', 'group'))
- update: bfloat16 [176, 1024, 768], P(None, ('dp', 'group'))
- new_weight: bfloat16 [176, 1024, 768], P(None, ('dp', 'group'))
The draws below stay inside these ranges and needn't reach their ends.
All inputs are finite; a program needn't handle non-finite values.
Results may differ from the reference program's by a relative error of at most 0.0088.
Values may be sent and summed in bfloat16 or wider, within the bound.
A program may use at most 64 MiB of HBM per device.

```python
import math
import jax
import jax.numpy as jnp
from jax import lax

ROWS = 1024
COLS = 768
ITERS = 2
MATS = 176


def spread_scales(key):
    row_key, column_key = jax.random.split(key)
    row_scale = jnp.exp(jax.random.uniform(row_key, (MATS, ROWS, 1), jnp.float32) * math.log(10.0))
    column_scale = jnp.exp(jax.random.uniform(column_key, (MATS, 1, COLS), jnp.float32) * math.log(10.0))
    return row_scale * column_scale * 0.1


def draw_gradient(key, part):
    key = jax.random.fold_in(key, 11)
    scale_key, noise_key = jax.random.split(key, 2)
    noise = jnp.clip(jax.random.normal(noise_key, (MATS, ROWS, COLS), jnp.float32), -5.0, 5.0)
    return noise * spread_scales(scale_key)


def draw_momentum(key, part):
    key = jax.random.fold_in(key, 23)
    scale_key, noise_key = jax.random.split(key, 2)
    noise = jnp.clip(jax.random.normal(noise_key, (MATS, ROWS, COLS), jnp.float32), -5.0, 5.0)
    return noise * spread_scales(scale_key)


def shard_levels(own_key, dims, pieces, low, high):
    level = 1.0
    for position, shards_of in pieces:
        heights = jax.random.uniform(jax.random.fold_in(jax.random.fold_in(own_key, 6), position), (shards_of,), jnp.float32, low / len(pieces), high / len(pieces))
        level = level * jnp.repeat(jnp.exp(heights), dims[position] // shards_of).reshape((-1,) + (1,) * (len(dims) - 1 - position))
    return level


def centred(rng, extent, width, reach, cuts=(), kind=jnp.bfloat16):
    loudness = shard_levels(rng, extent, cuts, -0.22, 0.18) if cuts else 1.0
    array = jax.random.normal(rng, extent, jnp.float32) * width * loudness
    return jnp.minimum(jnp.maximum(array, -reach), reach).astype(kind)


def setup_inputs(seed: int = 0) -> dict:
    key_list = jax.random.split(jax.random.key(seed), 4)
    return {
        "gradient": draw_gradient(jax.random.fold_in(key_list[3], 71), 0),
        "momentum": draw_momentum(jax.random.fold_in(key_list[3], 71), 0),
        "weight": centred(key_list[2], (MATS, ROWS, COLS), COLS ** -0.5, 0.21875, ((1, 512),)),
    }


momentum_decay = 0.95
coef_first = 3.4445
coef_second = -4.775
coef_third = 2.0315
epsilon_norm = 1e-07
learning_rate = 0.02
weight_decay = 0.1
rms_match = 0.2

def orthogonalize(matrix):
    values = matrix.astype(jnp.float32)
    frobenius = jnp.sqrt(jnp.sum(values * values))
    current = (values / (frobenius + epsilon_norm)).astype(jnp.bfloat16)
    for iteration in range(ITERS):
        gram_matrix = lax.dot_general(current, current, (((0,), (0,)), ((), ())), preferred_element_type=jnp.float32).astype(jnp.bfloat16)
        squared = jnp.dot(gram_matrix, gram_matrix, preferred_element_type=jnp.float32)
        polynomial = (coef_second * gram_matrix.astype(jnp.float32) + coef_third * squared).astype(jnp.bfloat16)
        current = (coef_first * current.astype(jnp.float32) + jnp.dot(current, polynomial, preferred_element_type=jnp.float32)).astype(jnp.bfloat16)
    return current

def reference(gradient, momentum, weight):
    new_momentum = momentum_decay * momentum + gradient
    advance = (gradient + momentum_decay * new_momentum).astype(jnp.bfloat16)
    orthogonal = lax.map(orthogonalize, advance)
    factor = rms_match * math.sqrt(max(ROWS, COLS))
    update = (factor * orthogonal.astype(jnp.float32)).astype(jnp.bfloat16)
    new_weight = ((1.0 - learning_rate * weight_decay) * weight.astype(jnp.float32) - learning_rate * update.astype(jnp.float32)).astype(jnp.bfloat16)
    return (new_momentum, update, new_weight)
```

```python
import math

import jax
import jax.numpy as jnp
from jax import lax
from jax.experimental import pallas as pl
from jax.experimental.pallas import tpu as pltpu
from jax.sharding import PartitionSpec as P

ROWS = 1024
COLS = 768
ITERS = 2
MATS = 176
DEVICES = 512

momentum_decay = 0.95
coef_first = 3.4445
coef_second = -4.775
coef_third = 2.0315
epsilon_norm = 1e-07
learning_rate = 0.02
weight_decay = 0.1
rms_match = 0.2

MESH = pl.DeviceIdType.MESH
TILE = 256
STEP = 16


def owner_of(t):
    x = lax.rem(t, 4)
    r = lax.div(t, 4)
    pair = lax.div(r, 11)
    k = lax.rem(r, 11)
    six = k < 6
    kk = jnp.where(six, k, k - 6)
    parity = lax.rem(x, 2)
    y = 2 * pair + jnp.where(six, parity, 1 - parity)
    skip = jnp.where(jnp.logical_and(jnp.logical_not(six), kk >= 4), 1, 0)
    d = kk + 1 + jnp.where(kk >= 2, 1, 0) + skip
    z = lax.rem(y + d + 2 * x, 8)
    return (y * 8 + z) * 2, x


def matrix_of(dp, x):
    core = lax.rem(dp, 2)
    place = lax.div(dp, 2)
    y = lax.div(place, 8)
    z = lax.rem(place, 8)
    d = lax.rem(z - y - 2 * x + 16, 8)
    six = lax.rem(y, 2) == lax.rem(x, 2)
    gap = jnp.logical_or(d == 0, d == 3)
    gap = jnp.logical_or(gap, jnp.logical_and(jnp.logical_not(six), d == 6))
    owns = jnp.logical_and(core == 0, jnp.logical_not(gap))
    kk = d - 1 - jnp.where(d >= 4, 1, 0)
    kk = kk - jnp.where(jnp.logical_and(jnp.logical_not(six), d >= 7), 1, 0)
    k = jnp.where(six, kk, kk + 6)
    t = (lax.div(y, 2) * 11 + k) * 4 + x
    return owns, jnp.where(owns, t, 0)


def dot_first(a, b):
    return lax.dot_general(a, b, (((0,), (0,)), ((), ())), preferred_element_type=jnp.float32)


def kernel(
    gradient, momentum, weight,
    new_momentum, update, new_weight,
    g_buf, m_buf, w_buf, nm_buf, advance, arrived, current, after, gram, poly, finished, returned, nw_buf,
    load_sem, store_sem, own_sem, send_sem, recv_sem, back_send, back_recv,
):
    dp = lax.axis_index("dp")
    x = lax.axis_index("group")
    me = dp * 4 + x
    owns, mine = matrix_of(dp, x)
    barrier = pltpu.get_barrier_semaphore()

    @pl.when(owns)
    def _():
        @pl.loop(1, DEVICES)
        def _(j):
            r = lax.rem(me + j, DEVICES)
            pl.semaphore_signal(barrier, inc=1, device_id=(lax.div(r, 4), lax.rem(r, 4)), device_id_type=MESH)

    loads = [
        pltpu.make_async_copy(gradient, g_buf, load_sem.at[0]),
        pltpu.make_async_copy(momentum, m_buf, load_sem.at[1]),
        pltpu.make_async_copy(weight, w_buf, load_sem.at[2]),
    ]
    for c in loads:
        c.start()
    for c in loads:
        c.wait()

    def mix(i, _):
        s = pl.ds(pl.multiple_of(i * STEP, STEP), STEP)
        g = g_buf[s]
        nm = momentum_decay * m_buf[s] + g
        nm_buf[s] = nm
        advance[s] = (g + momentum_decay * nm).astype(jnp.bfloat16)
        return 0

    lax.fori_loop(0, MATS // STEP, mix, 0)
    keep_momentum = pltpu.make_async_copy(nm_buf, new_momentum, store_sem.at[0])
    keep_momentum.start()

    own_count = jnp.where(owns, 1, 0)
    pl.semaphore_wait(barrier, MATS - own_count)

    shift = dp * 7 + x * 44

    @pl.loop(0, MATS)
    def _(k):
        t = lax.rem(k + shift, MATS)
        there = owner_of(t)

        @pl.when(jnp.logical_or(there[0] != dp, there[1] != x))
        def _():
            pltpu.make_async_remote_copy(
                src_ref=advance.at[t], dst_ref=arrived.at[me], send_sem=send_sem, recv_sem=recv_sem,
                device_id=there, device_id_type=MESH,
            ).start()

    @pl.when(owns)
    def _():
        own = pltpu.make_async_copy(advance.at[mine], arrived.at[me], own_sem.at[0])
        own.start()
        own.wait()
        pltpu.make_async_copy(
            arrived.at[pl.ds(0, DEVICES - 1)], arrived.at[pl.ds(0, DEVICES - 1)], recv_sem
        ).wait()

        def gather(i, total):
            block = arrived[pl.ds(pl.multiple_of(i * 32, 32), 32)].reshape(64, COLS)
            current[pl.ds(pl.multiple_of(i * 64, 64), 64), :] = block
            v = block.astype(jnp.float32)
            return total + jnp.sum(v * v)

        total = lax.fori_loop(0, DEVICES // 32, gather, jnp.float32(0))
        norm = jnp.sqrt(jnp.full((1, 1), total, jnp.float32)) + epsilon_norm

        def scale(i, _):
            s = pl.ds(pl.multiple_of(i * 64, 64), 64)
            current[s, :] = (current[s, :].astype(jnp.float32) / norm).astype(jnp.bfloat16)
            return 0

        lax.fori_loop(0, ROWS // 64, scale, 0)

        def make_poly(source):
            for j in range(COLS // TILE):
                c = slice(j * TILE, (j + 1) * TILE)
                gram[:, c] = dot_first(source[...], source[:, c]).astype(jnp.bfloat16)
            for j in range(COLS // TILE):
                c = slice(j * TILE, (j + 1) * TILE)
                squared = jnp.dot(gram[...], gram[:, c], preferred_element_type=jnp.float32)
                poly[:, c] = (coef_second * gram[:, c].astype(jnp.float32) + coef_third * squared).astype(
                    jnp.bfloat16
                )

        make_poly(current)
        for i in range(ROWS // TILE):
            r = slice(i * TILE, (i + 1) * TILE)
            product = jnp.dot(current[r, :], poly[...], preferred_element_type=jnp.float32)
            after[r, :] = (coef_first * current[r, :].astype(jnp.float32) + product).astype(jnp.bfloat16)
        make_poly(after)
        factor = rms_match * math.sqrt(max(ROWS, COLS))

        def finish(i, _):
            plane = lax.rem(i + lax.div(dp, 16), 8)
            r = pl.ds(pl.multiple_of(plane * 128, 128), 128)
            rows = after[r, :]
            product = jnp.dot(rows, poly[...], preferred_element_type=jnp.float32)
            rows = (coef_first * rows.astype(jnp.float32) + product).astype(jnp.bfloat16)
            rows = (factor * rows.astype(jnp.float32)).astype(jnp.bfloat16)
            finished[pl.ds(pl.multiple_of(plane * 64, 64), 64)] = rows.reshape(64, 2, COLS)

            @pl.loop(0, 64)
            def _(k):
                to = plane * 64 + lax.rem(me + k * 5, 64)

                @pl.when(to != me)
                def _():
                    pltpu.make_async_remote_copy(
                        src_ref=finished.at[to], dst_ref=returned.at[mine],
                        send_sem=back_send, recv_sem=back_recv,
                        device_id=(lax.div(to, 4), lax.rem(to, 4)), device_id_type=MESH,
                    ).start()

            return 0

        lax.fori_loop(0, 8, finish, 0)
        own_back = pltpu.make_async_copy(finished.at[me], returned.at[mine], own_sem.at[1])
        own_back.start()
        own_back.wait()
        pltpu.make_async_copy(
            advance.at[pl.ds(0, MATS - 1)], advance.at[pl.ds(0, MATS - 1)], send_sem
        ).wait()
        pltpu.make_async_copy(
            returned.at[pl.ds(0, MATS - 1)], returned.at[pl.ds(0, MATS - 1)], back_recv
        ).wait()
        pltpu.make_async_copy(
            finished.at[pl.ds(0, DEVICES - 1)], finished.at[pl.ds(0, DEVICES - 1)], back_send
        ).wait()

    @pl.when(jnp.logical_not(owns))
    def _():
        pltpu.make_async_copy(advance, advance, send_sem).wait()
        pltpu.make_async_copy(returned, returned, back_recv).wait()

    keep_update = pltpu.make_async_copy(returned, update, store_sem.at[1])
    keep_update.start()

    def step(i, _):
        s = pl.ds(pl.multiple_of(i * STEP, STEP), STEP)
        nw_buf[s] = (
            (1.0 - learning_rate * weight_decay) * w_buf[s].astype(jnp.float32)
            - learning_rate * returned[s].astype(jnp.float32)
        ).astype(jnp.bfloat16)
        return 0

    lax.fori_loop(0, MATS // STEP, step, 0)
    keep_weight = pltpu.make_async_copy(nw_buf, new_weight, store_sem.at[2])
    keep_weight.start()
    keep_momentum.wait()
    keep_update.wait()
    keep_weight.wait()


def per_device(gradient, momentum, weight):
    shape = gradient.shape
    f32, bf16 = jnp.float32, jnp.bfloat16
    blocks = (DEVICES,) + shape[1:]
    return pl.pallas_call(
        kernel,
        out_shape=(
            jax.ShapeDtypeStruct(shape, f32),
            jax.ShapeDtypeStruct(shape, bf16),
            jax.ShapeDtypeStruct(shape, bf16),
        ),
        in_specs=[pl.BlockSpec(memory_space=pl.ANY)] * 3,
        out_specs=[pl.BlockSpec(memory_space=pl.ANY)] * 3,
        scratch_shapes=[
            pltpu.VMEM(shape, f32),
            pltpu.VMEM(shape, f32),
            pltpu.VMEM(shape, bf16),
            pltpu.VMEM(shape, f32),
            pltpu.VMEM(shape, bf16),
            pltpu.VMEM(blocks, bf16),
            pltpu.VMEM((ROWS, COLS), bf16),
            pltpu.VMEM((ROWS, COLS), bf16),
            pltpu.VMEM((COLS, COLS), bf16),
            pltpu.VMEM((COLS, COLS), bf16),
            pltpu.VMEM(blocks, bf16),
            pltpu.VMEM(shape, bf16),
            pltpu.VMEM(shape, bf16),
            pltpu.SemaphoreType.DMA((3,)),
            pltpu.SemaphoreType.DMA((3,)),
            pltpu.SemaphoreType.DMA((2,)),
            pltpu.SemaphoreType.DMA,
            pltpu.SemaphoreType.DMA,
            pltpu.SemaphoreType.DMA,
            pltpu.SemaphoreType.DMA,
        ],
        compiler_params=pltpu.CompilerParams(
            collective_id=0, has_side_effects=True, vmem_limit_bytes=48 * 2**20
        ),
    )(gradient, momentum, weight)


def solution(mesh):
    spec = P(None, ("dp", "group"), None)
    return jax.shard_map(
        per_device, mesh=mesh, in_specs=(spec, spec, spec), out_specs=(spec, spec, spec), check_vma=False
    )
```

```python
import math

import jax
import jax.numpy as jnp
from jax import lax
from jax.experimental import pallas as pl
from jax.experimental.pallas import tpu as pltpu
from jax.sharding import PartitionSpec as P

ROWS = 1024
COLS = 768
ITERS = 2
MATS = 176
DEVICES = 512

momentum_decay = 0.95
coef_first = 3.4445
coef_second = -4.775
coef_third = 2.0315
epsilon_norm = 1e-07
learning_rate = 0.02
weight_decay = 0.1
rms_match = 0.2

MESH = pl.DeviceIdType.MESH
TILE = 256
STEP = 16
FAR = (4, 3, 5, 2, 6, 1, 7, 0)


def offset_of(k):
    six = k < 6
    kk = jnp.where(six, k, k - 6)
    last = jnp.logical_and(jnp.logical_not(six), kk >= 4)
    return six, kk + 1 + jnp.where(kk >= 2, 1, 0) + jnp.where(last, 1, 0)


def owner_of(q, six, d):
    x = lax.div(q, 4)
    parity = lax.rem(x, 2)
    y = 2 * lax.rem(q, 4) + jnp.where(six, parity, 1 - parity)
    z = lax.rem(y + d + 2 * x, 8)
    return (y * 8 + z) * 2, x


def matrix_of(dp, x):
    core = lax.rem(dp, 2)
    place = lax.div(dp, 2)
    y = lax.div(place, 8)
    z = lax.rem(place, 8)
    d = lax.rem(z - y - 2 * x + 16, 8)
    six = lax.rem(y, 2) == lax.rem(x, 2)
    gap = jnp.logical_or(d == 0, d == 3)
    gap = jnp.logical_or(gap, jnp.logical_and(jnp.logical_not(six), d == 6))
    owns = jnp.logical_and(core == 0, jnp.logical_not(gap))
    kk = d - 1 - jnp.where(d >= 4, 1, 0)
    kk = kk - jnp.where(jnp.logical_and(jnp.logical_not(six), d >= 7), 1, 0)
    k = jnp.where(six, kk, kk + 6)
    t = k * 16 + x * 4 + lax.div(y, 2)
    return owns, jnp.where(owns, t, 0)


def far_first(a):
    half = lax.div(a, 2)
    return jnp.where(lax.rem(a, 2) == 0, 4 - half, lax.rem(5 + half, 8))


def dot_first(a, b):
    return lax.dot_general(a, b, (((0,), (0,)), ((), ())), preferred_element_type=jnp.float32)


def make_gram(source, gram, norm):
    scale = None
    blocks = []
    for i in range(COLS // TILE):
        a = i * TILE
        blocks.append(dot_first(source[:, a : a + TILE], source[:, a:]))
    if norm:
        row = lax.broadcasted_iota(jnp.int32, (TILE, TILE), 0)
        column = lax.broadcasted_iota(jnp.int32, (TILE, TILE), 1)
        trace = jnp.zeros((1, 1), jnp.float32)
        for block in blocks:
            diagonal = jnp.where(row == column, block[:, :TILE], 0.0)
            trace = trace + jnp.sum(diagonal, axis=(0, 1), keepdims=True)
        scale = 1.0 / (jnp.sqrt(trace) + epsilon_norm)
        blocks = [(block * scale) * scale for block in blocks]
    for i, block in enumerate(blocks):
        a = i * TILE
        block = block.astype(jnp.bfloat16)
        gram[a : a + TILE, a:] = block
        for j in range(i + 1, COLS // TILE):
            gram[j * TILE : (j + 1) * TILE, a : a + TILE] = block[:, (j - i) * TILE : (j - i + 1) * TILE].T
    return scale


def make_poly(gram, poly):
    for i in range(COLS // TILE):
        a = i * TILE
        squared = jnp.dot(gram[a : a + TILE, :], gram[:, a:], preferred_element_type=jnp.float32)
        block = (coef_second * gram[a : a + TILE, a:].astype(jnp.float32) + coef_third * squared).astype(jnp.bfloat16)
        poly[a : a + TILE, a:] = block
        for j in range(i + 1, COLS // TILE):
            poly[j * TILE : (j + 1) * TILE, a : a + TILE] = block[:, (j - i) * TILE : (j - i + 1) * TILE].T


def kernel(
    gradient, momentum, weight,
    new_momentum, update, new_weight,
    g_buf, m_buf, w_buf, nm_buf, advance, arrived, current, after, gram, poly, finished, returned, nw_buf,
    ready, load_sem, store_sem, own_sem, send_sem, recv_sem, back_send, back_recv,
):
    dp = lax.axis_index("dp")
    x = lax.axis_index("group")
    me = dp * 4 + x
    owns, mine = matrix_of(dp, x)
    barrier = pltpu.get_barrier_semaphore()

    place = lax.div(dp, 2)
    core = lax.rem(dp, 2)
    y, z = lax.div(place, 8), lax.rem(place, 8)

    loads = [
        pltpu.make_async_copy(gradient, g_buf, load_sem.at[0]),
        pltpu.make_async_copy(momentum, m_buf, load_sem.at[1]),
        pltpu.make_async_copy(weight, w_buf, load_sem.at[2]),
    ]
    for c in loads:
        c.start()
    @pl.when(core == 1)
    def _():
        pl.semaphore_signal(barrier, inc=1, device_id=(dp - 1, x), device_id_type=MESH)

    @pl.when(owns)
    def _():
        planes = [lax.rem(y + dy, 8) * 16 for dy in FAR]
        groups = [lax.rem(x + dx, 4) for dx in (2, 1, 3, 0)]

        @pl.loop(0, 8)
        def _(j):
            along = lax.rem(z + far_first(j), 8) * 2
            for plane in planes:
                for tx in groups:
                    if plane is planes[-1] and tx is groups[-1]:

                        @pl.when(j != 7)
                        def _():
                            pl.semaphore_signal(
                                barrier, inc=1, device_id=(plane + along, tx), device_id_type=MESH
                            )

                    else:
                        pl.semaphore_signal(barrier, inc=1, device_id=(plane + along, tx), device_id_type=MESH)

    for c in loads:
        c.wait()

    def mix(i, _):
        s = pl.ds(pl.multiple_of(i * STEP, STEP), STEP)
        g = g_buf[s]
        nm = momentum_decay * m_buf[s] + g
        nm_buf[s] = nm
        advance[s] = (g + momentum_decay * nm).astype(jnp.bfloat16)
        return 0

    lax.fori_loop(0, MATS // STEP, mix, 0)
    keep_momentum = pltpu.make_async_copy(nm_buf, new_momentum, store_sem.at[0])
    keep_momentum.start()

    own_count = jnp.where(owns, 1, 0)
    @pl.when(core == 0)
    def _():
        pl.semaphore_wait(barrier, MATS + 1 - own_count)
        pl.semaphore_signal(ready, inc=1, device_id=(dp + 1, x), device_id_type=MESH)

    @pl.when(core == 1)
    def _():
        pl.semaphore_wait(ready, 1)

    def send_to(count, first, turn):
        @pl.loop(0, count)
        def _(i):
            k = first + 2 * lax.rem(i + turn, count)
            six, d = offset_of(k)
            odd = jnp.where(six, 0, 1)
            for tx in range(4):
                ty = 1 - odd if tx % 2 else odd
                tz = lax.rem(ty + d + 2 * tx, 8)
                for pair in range(4):
                    there = ((2 * pair + ty) * 8 + tz) * 2
                    t = k * 16 + tx * 4 + pair

                    @pl.when(jnp.logical_or(there != dp, x != tx))
                    def _():
                        pltpu.make_async_remote_copy(
                            src_ref=advance.at[t], dst_ref=arrived.at[me], send_sem=send_sem, recv_sem=recv_sem,
                            device_id=(there, tx), device_id_type=MESH,
                        ).start()

                    tz = tz + 2
                    tz = jnp.where(tz >= 8, tz - 8, tz)

    send_to(6, 0, z)
    send_to(5, 1, z)

    @pl.when(owns)
    def _():
        own = pltpu.make_async_copy(advance.at[mine], arrived.at[me], own_sem.at[0])
        own.start()
        own.wait()
        pltpu.make_async_copy(
            arrived.at[pl.ds(0, DEVICES - 1)], arrived.at[pl.ds(0, DEVICES - 1)], recv_sem
        ).wait()

        def gather(i, _):
            block = arrived[pl.ds(pl.multiple_of(i * 32, 32), 32)].reshape(64, COLS)
            current[pl.ds(pl.multiple_of(i * 64, 64), 64), :] = block
            return 0

        lax.fori_loop(0, DEVICES // 32, gather, 0)
        scale = make_gram(current, gram, True)
        make_poly(gram, poly)
        for i in range(ROWS // TILE):
            r = slice(i * TILE, (i + 1) * TILE)
            product = jnp.dot(current[r, :], poly[...], preferred_element_type=jnp.float32)
            after[r, :] = (scale * (coef_first * current[r, :].astype(jnp.float32) + product)).astype(jnp.bfloat16)
        make_gram(after, gram, False)
        make_poly(gram, poly)
        factor = rms_match * math.sqrt(max(ROWS, COLS))

        groups = [lax.rem(x + dx, 4) for dx in (2, 1, 3, 0)]

        def finish(i, _):
            plane = lax.rem(y + far_first(i), 8)
            r = pl.ds(pl.multiple_of(plane * 128, 128), 128)
            rows = after[r, :]
            product = jnp.dot(rows, poly[...], preferred_element_type=jnp.float32)
            rows = (coef_first * rows.astype(jnp.float32) + product).astype(jnp.bfloat16)
            rows = (factor * rows.astype(jnp.float32)).astype(jnp.bfloat16)
            finished[pl.ds(pl.multiple_of(plane * 64, 64), 64)] = rows.reshape(64, 2, COLS)

            @pl.loop(0, 8)
            def _(j):
                there = (plane * 8 + lax.rem(z + far_first(j), 8)) * 2
                for way in range(8):
                    tx = groups[way % 4]
                    td = there + way // 4

                    @pl.when(jnp.logical_or(td != dp, tx != x))
                    def _():
                        pltpu.make_async_remote_copy(
                            src_ref=finished.at[td * 4 + tx], dst_ref=returned.at[mine],
                            send_sem=back_send, recv_sem=back_recv, device_id=(td, tx), device_id_type=MESH,
                        ).start()

            return 0

        lax.fori_loop(0, 8, finish, 0)
        own_back = pltpu.make_async_copy(finished.at[me], returned.at[mine], own_sem.at[1])
        own_back.start()
        own_back.wait()
        pltpu.make_async_copy(
            advance.at[pl.ds(0, MATS - 1)], advance.at[pl.ds(0, MATS - 1)], send_sem
        ).wait()
        pltpu.make_async_copy(
            returned.at[pl.ds(0, MATS - 1)], returned.at[pl.ds(0, MATS - 1)], back_recv
        ).wait()
        pltpu.make_async_copy(
            finished.at[pl.ds(0, DEVICES - 1)], finished.at[pl.ds(0, DEVICES - 1)], back_send
        ).wait()

    @pl.when(jnp.logical_not(owns))
    def _():
        pltpu.make_async_copy(advance, advance, send_sem).wait()
        pltpu.make_async_copy(returned, returned, back_recv).wait()

    keep_update = pltpu.make_async_copy(returned, update, store_sem.at[1])
    keep_update.start()

    def step(i, _):
        s = pl.ds(pl.multiple_of(i * STEP, STEP), STEP)
        nw_buf[s] = (
            (1.0 - learning_rate * weight_decay) * w_buf[s].astype(jnp.float32)
            - learning_rate * returned[s].astype(jnp.float32)
        ).astype(jnp.bfloat16)
        return 0

    lax.fori_loop(0, MATS // STEP, step, 0)
    keep_weight = pltpu.make_async_copy(nw_buf, new_weight, store_sem.at[2])
    keep_weight.start()
    keep_momentum.wait()
    keep_update.wait()
    keep_weight.wait()


def per_device(gradient, momentum, weight):
    shape = gradient.shape
    f32, bf16 = jnp.float32, jnp.bfloat16
    blocks = (DEVICES,) + shape[1:]
    return pl.pallas_call(
        kernel,
        out_shape=(
            jax.ShapeDtypeStruct(shape, f32),
            jax.ShapeDtypeStruct(shape, bf16),
            jax.ShapeDtypeStruct(shape, bf16),
        ),
        in_specs=[pl.BlockSpec(memory_space=pltpu.HBM)] * 3,
        out_specs=[pl.BlockSpec(memory_space=pl.ANY)] * 3,
        scratch_shapes=[
            pltpu.VMEM(shape, f32),
            pltpu.VMEM(shape, f32),
            pltpu.VMEM(shape, bf16),
            pltpu.VMEM(shape, f32),
            pltpu.VMEM(shape, bf16),
            pltpu.VMEM(blocks, bf16),
            pltpu.VMEM((ROWS, COLS), bf16),
            pltpu.VMEM((ROWS, COLS), bf16),
            pltpu.VMEM((COLS, COLS), bf16),
            pltpu.VMEM((COLS, COLS), bf16),
            pltpu.VMEM(blocks, bf16),
            pltpu.VMEM(shape, bf16),
            pltpu.VMEM(shape, bf16),
            pltpu.SemaphoreType.REGULAR,
            pltpu.SemaphoreType.DMA((3,)),
            pltpu.SemaphoreType.DMA((3,)),
            pltpu.SemaphoreType.DMA((2,)),
            pltpu.SemaphoreType.DMA,
            pltpu.SemaphoreType.DMA,
            pltpu.SemaphoreType.DMA,
            pltpu.SemaphoreType.DMA,
        ],
        compiler_params=pltpu.CompilerParams(
            collective_id=0, has_side_effects=True, vmem_limit_bytes=48 * 2**20
        ),
    )(gradient, momentum, weight)


def solution(mesh):
    spec = P(None, ("dp", "group"), None)
    return jax.shard_map(
        per_device, mesh=mesh, in_specs=(spec, spec, spec), out_specs=(spec, spec, spec), check_vma=False
    )
```

```python
import math

import jax
import jax.numpy as jnp
from jax import lax
from jax.experimental import pallas as pl
from jax.experimental.pallas import tpu as pltpu
from jax.sharding import PartitionSpec as P

ROWS = 1024
COLS = 768
ITERS = 2
MATS = 176
DEVICES = 512

momentum_decay = 0.95
coef_first = 3.4445
coef_second = -4.775
coef_third = 2.0315
epsilon_norm = 1e-07
learning_rate = 0.02
weight_decay = 0.1
rms_match = 0.2

MESH = pl.DeviceIdType.MESH
TILE = 256
STEP = 16
PARTS = 4
FAR = (4, 3, 5, 2, 6, 1, 7, 0)


def offset_of(k):
    six = k < 6
    kk = jnp.where(six, k, k - 6)
    last = jnp.logical_and(jnp.logical_not(six), kk >= 4)
    return six, kk + 1 + jnp.where(kk >= 2, 1, 0) + jnp.where(last, 1, 0)


def owner_of(q, six, d):
    x = lax.div(q, 4)
    parity = lax.rem(x, 2)
    y = 2 * lax.rem(q, 4) + jnp.where(six, parity, 1 - parity)
    z = lax.rem(y + d + 2 * x, 8)
    return (y * 8 + z) * 2, x


def matrix_of(dp, x):
    core = lax.rem(dp, 2)
    place = lax.div(dp, 2)
    y = lax.div(place, 8)
    z = lax.rem(place, 8)
    d = lax.rem(z - y - 2 * x + 16, 8)
    six = lax.rem(y, 2) == lax.rem(x, 2)
    gap = jnp.logical_or(d == 0, d == 3)
    gap = jnp.logical_or(gap, jnp.logical_and(jnp.logical_not(six), d == 6))
    owns = jnp.logical_and(core == 0, jnp.logical_not(gap))
    kk = d - 1 - jnp.where(d >= 4, 1, 0)
    kk = kk - jnp.where(jnp.logical_and(jnp.logical_not(six), d >= 7), 1, 0)
    k = jnp.where(six, kk, kk + 6)
    t = k * 16 + x * 4 + lax.div(y, 2)
    return owns, jnp.where(owns, t, 0)


def far_first(a):
    half = lax.div(a, 2)
    return jnp.where(lax.rem(a, 2) == 0, 4 - half, lax.rem(5 + half, 8))


def dot_first(a, b):
    return lax.dot_general(a, b, (((0,), (0,)), ((), ())), preferred_element_type=jnp.float32)


def make_gram(source, gram, norm):
    scale = None
    blocks = []
    for i in range(COLS // TILE):
        a = i * TILE
        blocks.append(dot_first(source[:, a : a + TILE], source[:, a:]))
    if norm:
        row = lax.broadcasted_iota(jnp.int32, (TILE, TILE), 0)
        column = lax.broadcasted_iota(jnp.int32, (TILE, TILE), 1)
        trace = jnp.zeros((1, 1), jnp.float32)
        for block in blocks:
            diagonal = jnp.where(row == column, block[:, :TILE], 0.0)
            trace = trace + jnp.sum(diagonal, axis=(0, 1), keepdims=True)
        scale = 1.0 / (jnp.sqrt(trace) + epsilon_norm)
        blocks = [(block * scale) * scale for block in blocks]
    for i, block in enumerate(blocks):
        a = i * TILE
        block = block.astype(jnp.bfloat16)
        gram[a : a + TILE, a:] = block
        for j in range(i + 1, COLS // TILE):
            gram[j * TILE : (j + 1) * TILE, a : a + TILE] = block[:, (j - i) * TILE : (j - i + 1) * TILE].T
    return scale


def make_poly(gram, poly):
    for i in range(COLS // TILE):
        a = i * TILE
        squared = jnp.dot(gram[a : a + TILE, :], gram[:, a:], preferred_element_type=jnp.float32)
        block = (coef_second * gram[a : a + TILE, a:].astype(jnp.float32) + coef_third * squared).astype(jnp.bfloat16)
        poly[a : a + TILE, a:] = block
        for j in range(i + 1, COLS // TILE):
            poly[j * TILE : (j + 1) * TILE, a : a + TILE] = block[:, (j - i) * TILE : (j - i + 1) * TILE].T


def kernel(
    gradient, momentum,
    new_momentum, returned,
    g_buf, m_buf, nm_buf, advance, arrived, current, after, gram, poly, finished,
    ready, load_sem, store_sem, own_sem, send_sem, recv_sem, back_send, back_recv,
):
    dp = lax.axis_index("dp")
    x = lax.axis_index("group")
    me = dp * 4 + x
    owns, mine = matrix_of(dp, x)
    barrier = pltpu.get_barrier_semaphore()

    place = lax.div(dp, 2)
    core = lax.rem(dp, 2)
    y, z = lax.div(place, 8), lax.rem(place, 8)

    loads = [
        pltpu.make_async_copy(gradient, g_buf, load_sem.at[0]),
        pltpu.make_async_copy(momentum, m_buf, load_sem.at[1]),
    ]
    for c in loads:
        c.start()
    @pl.when(core == 1)
    def _():
        pl.semaphore_signal(barrier, inc=1, device_id=(dp - 1, x), device_id_type=MESH)

    @pl.when(owns)
    def _():
        planes = [lax.rem(y + dy, 8) * 16 for dy in FAR]
        groups = [lax.rem(x + dx, 4) for dx in (2, 1, 3, 0)]

        @pl.loop(0, 8)
        def _(j):
            along = lax.rem(z + far_first(j), 8) * 2
            for plane in planes:
                for tx in groups:
                    if plane is planes[-1] and tx is groups[-1]:

                        @pl.when(j != 7)
                        def _():
                            pl.semaphore_signal(
                                barrier, inc=1, device_id=(plane + along, tx), device_id_type=MESH
                            )

                    else:
                        pl.semaphore_signal(barrier, inc=1, device_id=(plane + along, tx), device_id_type=MESH)

    for c in loads:
        c.wait()

    def mix(i, _):
        s = pl.ds(pl.multiple_of(i * STEP, STEP), STEP)
        g = g_buf[s]
        nm = momentum_decay * m_buf[s] + g
        nm_buf[s] = nm
        advance[s] = (g + momentum_decay * nm).astype(jnp.bfloat16)
        return 0

    lax.fori_loop(0, MATS // STEP, mix, 0)
    keep_momentum = pltpu.make_async_copy(nm_buf, new_momentum, store_sem.at[0])
    keep_momentum.start()

    own_count = jnp.where(owns, 1, 0)
    @pl.when(core == 0)
    def _():
        pl.semaphore_wait(barrier, MATS + 1 - own_count)
        pl.semaphore_signal(ready, inc=1, device_id=(dp + 1, x), device_id_type=MESH)

    @pl.when(core == 1)
    def _():
        pl.semaphore_wait(ready, 1)

    slot = z * 64 + y * 8 + core * 4 + x

    def send_to(count, first, turn):
        @pl.loop(0, count)
        def _(i):
            k = first + 2 * lax.rem(i + turn, count)
            six, d = offset_of(k)
            odd = jnp.where(six, 0, 1)
            for tx in range(4):
                ty = 1 - odd if tx % 2 else odd
                tz = lax.rem(ty + d + 2 * tx, 8)
                for pair in range(4):
                    there = ((2 * pair + ty) * 8 + tz) * 2
                    t = k * 16 + tx * 4 + pair

                    @pl.when(jnp.logical_or(there != dp, x != tx))
                    def _():
                        pltpu.make_async_remote_copy(
                            src_ref=advance.at[t], dst_ref=arrived.at[slot], send_sem=send_sem, recv_sem=recv_sem,
                            device_id=(there, tx), device_id_type=MESH,
                        ).start()

                    tz = tz + 2
                    tz = jnp.where(tz >= 8, tz - 8, tz)

    send_to(6, 0, z)
    send_to(5, 1, z)

    @pl.when(owns)
    def _():
        own = pltpu.make_async_copy(advance.at[mine], arrived.at[slot], own_sem.at[0])
        own.start()
        own.wait()
        pltpu.make_async_copy(
            arrived.at[pl.ds(0, DEVICES - 1)], arrived.at[pl.ds(0, DEVICES - 1)], recv_sem
        ).wait()

        def gather(i, _):
            block = arrived[pl.ds(pl.multiple_of(i * 32, 32), 32)].reshape(64, COLS)
            current[pl.ds(pl.multiple_of(i * 64, 64), 64), :] = block
            return 0

        lax.fori_loop(0, DEVICES // 32, gather, 0)
        scale = make_gram(current, gram, True)
        make_poly(gram, poly)
        for i in range(ROWS // TILE):
            r = slice(i * TILE, (i + 1) * TILE)
            product = jnp.dot(current[r, :], poly[...], preferred_element_type=jnp.float32)
            after[r, :] = (scale * (coef_first * current[r, :].astype(jnp.float32) + product)).astype(jnp.bfloat16)
        make_gram(after, gram, False)
        make_poly(gram, poly)
        factor = rms_match * math.sqrt(max(ROWS, COLS))

        groups = [lax.rem(x + dx, 4) for dx in (2, 1, 3, 0)]

        def finish(i, _):
            plane = lax.div(i, 4) * 4 + lax.rem(z + i, 4)
            r = pl.ds(pl.multiple_of(plane * 128, 128), 128)
            rows = after[r, :]
            product = jnp.dot(rows, poly[...], preferred_element_type=jnp.float32)
            rows = (coef_first * rows.astype(jnp.float32) + product).astype(jnp.bfloat16)
            rows = (factor * rows.astype(jnp.float32)).astype(jnp.bfloat16)
            finished[pl.ds(pl.multiple_of(plane * 64, 64), 64)] = rows.reshape(64, 2, COLS)

            @pl.loop(0, 8)
            def _(j):
                ty = lax.rem(y + far_first(j), 8)
                there = (ty * 8 + plane) * 2
                row = plane * 64 + ty * 8
                for way in range(8):
                    tx = groups[way % 4]
                    td = there + way // 4

                    @pl.when(jnp.logical_or(td != dp, tx != x))
                    def _():
                        pltpu.make_async_remote_copy(
                            src_ref=finished.at[row + way // 4 * 4 + tx], dst_ref=returned.at[mine],
                            send_sem=back_send, recv_sem=back_recv, device_id=(td, tx), device_id_type=MESH,
                        ).start()

            return 0

        lax.fori_loop(0, 8, finish, 0)
        own_back = pltpu.make_async_copy(finished.at[slot], returned.at[mine], own_sem.at[1])
        own_back.start()
        own_back.wait()
        pltpu.make_async_copy(
            advance.at[pl.ds(0, MATS - 1)], advance.at[pl.ds(0, MATS - 1)], send_sem
        ).wait()
        pltpu.make_async_copy(
            returned.at[pl.ds(0, MATS - 1)], returned.at[pl.ds(0, MATS - 1)], back_recv
        ).wait()
        pltpu.make_async_copy(
            finished.at[pl.ds(0, DEVICES - 1)], finished.at[pl.ds(0, DEVICES - 1)], back_send
        ).wait()

    @pl.when(jnp.logical_not(owns))
    def _():
        pltpu.make_async_copy(advance, advance, send_sem).wait()
        pltpu.make_async_copy(returned, returned, back_recv).wait()

    keep_momentum.wait()


def last_step(new_momentum_in, update_in, weight, new_momentum, update, new_weight, u_buf, w_buf, nw_buf, nm_buf, part_sem):
    size = MATS // PARTS
    parts = [pl.ds(i * size, size) for i in range(PARTS)]
    loads = [
        (
            pltpu.make_async_copy(update_in.at[p], u_buf.at[p], part_sem.at[0, i]),
            pltpu.make_async_copy(weight.at[p], w_buf.at[p], part_sem.at[1, i]),
        )
        for i, p in enumerate(parts)
    ]
    for pair in loads:
        for c in pair:
            c.start()
    keeps = [pltpu.make_async_copy(new_momentum_in.at[p], nm_buf.at[p], part_sem.at[4, i]) for i, p in enumerate(parts)]
    for c in keeps:
        c.start()
    stores = []
    for i, p in enumerate(parts):
        for c in loads[i]:
            c.wait()
        stores.append(pltpu.make_async_copy(u_buf.at[p], update.at[p], part_sem.at[2, i]))
        stores[-1].start()

        def step(j, _):
            s = pl.ds(pl.multiple_of(i * size + j * (size // 2), size // 2), size // 2)
            nw_buf[s] = (
                (1.0 - learning_rate * weight_decay) * w_buf[s].astype(jnp.float32)
                - learning_rate * u_buf[s].astype(jnp.float32)
            ).astype(jnp.bfloat16)
            return 0

        lax.fori_loop(0, 2, step, 0)
        stores.append(pltpu.make_async_copy(nw_buf.at[p], new_weight.at[p], part_sem.at[3, i]))
        stores[-1].start()
        keeps[i].wait()
        stores.append(pltpu.make_async_copy(nm_buf.at[p], new_momentum.at[p], part_sem.at[5, i]))
        stores[-1].start()
    for c in stores:
        c.wait()


def per_device(gradient, momentum, weight):
    shape = gradient.shape
    f32, bf16 = jnp.float32, jnp.bfloat16
    blocks = (DEVICES,) + shape[1:]
    new_momentum, update = pl.pallas_call(
        kernel,
        out_shape=(jax.ShapeDtypeStruct(shape, f32), jax.ShapeDtypeStruct(shape, bf16)),
        in_specs=[pl.BlockSpec(memory_space=pl.ANY)] * 2,
        out_specs=[pl.BlockSpec(memory_space=pl.ANY)] * 2,
        scratch_shapes=[
            pltpu.VMEM(shape, f32),
            pltpu.VMEM(shape, f32),
            pltpu.VMEM(shape, f32),
            pltpu.VMEM(shape, bf16),
            pltpu.VMEM(blocks, bf16),
            pltpu.VMEM((ROWS, COLS), bf16),
            pltpu.VMEM((ROWS, COLS), bf16),
            pltpu.VMEM((COLS, COLS), bf16),
            pltpu.VMEM((COLS, COLS), bf16),
            pltpu.VMEM(blocks, bf16),
            pltpu.SemaphoreType.REGULAR,
            pltpu.SemaphoreType.DMA((2,)),
            pltpu.SemaphoreType.DMA((1,)),
            pltpu.SemaphoreType.DMA((2,)),
            pltpu.SemaphoreType.DMA,
            pltpu.SemaphoreType.DMA,
            pltpu.SemaphoreType.DMA,
            pltpu.SemaphoreType.DMA,
        ],
        compiler_params=pltpu.CompilerParams(
            collective_id=0, has_side_effects=True, vmem_limit_bytes=60 * 2**20
        ),
    )(gradient, momentum)
    return pl.pallas_call(
        last_step,
        out_shape=(
            jax.ShapeDtypeStruct(shape, f32),
            jax.ShapeDtypeStruct(shape, bf16),
            jax.ShapeDtypeStruct(shape, bf16),
        ),
        in_specs=[pl.BlockSpec(memory_space=pl.ANY)] * 3,
        out_specs=[pl.BlockSpec(memory_space=pl.ANY)] * 3,
        scratch_shapes=[pltpu.VMEM(shape, bf16)] * 3
        + [pltpu.VMEM(shape, f32), pltpu.SemaphoreType.DMA((6, PARTS))],
        compiler_params=pltpu.CompilerParams(vmem_limit_bytes=60 * 2**20),
    )(new_momentum, update, weight)


def solution(mesh):
    spec = P(None, ("dp", "group"), None)
    return jax.shard_map(
        per_device, mesh=mesh, in_specs=(spec, spec, spec), out_specs=(spec, spec, spec), check_vma=False
    )
```

```python
import math

import jax
import jax.numpy as jnp
from jax import lax
from jax.experimental import pallas as pl
from jax.experimental.pallas import tpu as pltpu
from jax.sharding import PartitionSpec as P

ROWS = 1024
COLS = 768
ITERS = 2
MATS = 176
DEVICES = 512

momentum_decay = 0.95
coef_first = 3.4445
coef_second = -4.775
coef_third = 2.0315
epsilon_norm = 1e-07
learning_rate = 0.02
weight_decay = 0.1
rms_match = 0.2

MESH = pl.DeviceIdType.MESH
TILE = 256
STEP = 16
PARTS = 4
FAR = (4, 3, 5, 2, 6, 1, 7, 0)


def offset_of(k):
    six = k < 6
    kk = jnp.where(six, k, k - 6)
    last = jnp.logical_and(jnp.logical_not(six), kk >= 4)
    return six, kk + 1 + jnp.where(kk >= 2, 1, 0) + jnp.where(last, 1, 0)


def owner_of(q, six, d):
    x = lax.div(q, 4)
    parity = lax.rem(x, 2)
    y = 2 * lax.rem(q, 4) + jnp.where(six, parity, 1 - parity)
    z = lax.rem(y + d + 2 * x, 8)
    return (y * 8 + z) * 2, x


def matrix_of(dp, x):
    core = lax.rem(dp, 2)
    place = lax.div(dp, 2)
    y = lax.div(place, 8)
    z = lax.rem(place, 8)
    d = lax.rem(z - y - 2 * x + 16, 8)
    six = lax.rem(y, 2) == lax.rem(x, 2)
    gap = jnp.logical_or(d == 0, d == 3)
    gap = jnp.logical_or(gap, jnp.logical_and(jnp.logical_not(six), d == 6))
    owns = jnp.logical_and(core == 0, jnp.logical_not(gap))
    kk = d - 1 - jnp.where(d >= 4, 1, 0)
    kk = kk - jnp.where(jnp.logical_and(jnp.logical_not(six), d >= 7), 1, 0)
    k = jnp.where(six, kk, kk + 6)
    t = k * 16 + x * 4 + lax.div(y, 2)
    return owns, jnp.where(owns, t, 0)


def far_first(a):
    half = lax.div(a, 2)
    return jnp.where(lax.rem(a, 2) == 0, 4 - half, lax.rem(5 + half, 8))


def dot_first(a, b):
    return lax.dot_general(a, b, (((0,), (0,)), ((), ())), preferred_element_type=jnp.float32)


def make_gram(source, gram, norm):
    scale = None
    blocks = []
    for i in range(COLS // TILE):
        a = i * TILE
        blocks.append(dot_first(source[:, a : a + TILE], source[:, a:]))
    if norm:
        row = lax.broadcasted_iota(jnp.int32, (TILE, TILE), 0)
        column = lax.broadcasted_iota(jnp.int32, (TILE, TILE), 1)
        trace = jnp.zeros((1, 1), jnp.float32)
        for block in blocks:
            diagonal = jnp.where(row == column, block[:, :TILE], 0.0)
            trace = trace + jnp.sum(diagonal, axis=(0, 1), keepdims=True)
        scale = 1.0 / (jnp.sqrt(trace) + epsilon_norm)
        blocks = [(block * scale) * scale for block in blocks]
    for i, block in enumerate(blocks):
        a = i * TILE
        block = block.astype(jnp.bfloat16)
        gram[a : a + TILE, a:] = block
        for j in range(i + 1, COLS // TILE):
            gram[j * TILE : (j + 1) * TILE, a : a + TILE] = block[:, (j - i) * TILE : (j - i + 1) * TILE].T
    return scale


def make_poly(gram, poly):
    for i in range(COLS // TILE):
        a = i * TILE
        squared = jnp.dot(gram[a : a + TILE, :], gram[:, a:], preferred_element_type=jnp.float32)
        block = (coef_second * gram[a : a + TILE, a:].astype(jnp.float32) + coef_third * squared).astype(jnp.bfloat16)
        poly[a : a + TILE, a:] = block
        for j in range(i + 1, COLS // TILE):
            poly[j * TILE : (j + 1) * TILE, a : a + TILE] = block[:, (j - i) * TILE : (j - i + 1) * TILE].T


def kernel(
    gradient, momentum,
    new_momentum, returned,
    g_buf, m_buf, nm_buf, advance, arrived, current, after, gram, poly, finished,
    ready, load_sem, store_sem, own_sem, send_sem, recv_sem, back_send, back_recv,
):
    dp = lax.axis_index("dp")
    x = lax.axis_index("group")
    me = dp * 4 + x
    owns, mine = matrix_of(dp, x)
    barrier = pltpu.get_barrier_semaphore()

    place = lax.div(dp, 2)
    core = lax.rem(dp, 2)
    y, z = lax.div(place, 8), lax.rem(place, 8)

    loads = [
        pltpu.make_async_copy(gradient, g_buf, load_sem.at[0]),
        pltpu.make_async_copy(momentum, m_buf, load_sem.at[1]),
    ]
    for c in loads:
        c.start()
    @pl.when(core == 1)
    def _():
        pl.semaphore_signal(barrier, inc=1, device_id=(dp - 1, x), device_id_type=MESH)

    @pl.when(owns)
    def _():
        planes = [lax.rem(y + dy, 8) * 16 for dy in FAR]
        groups = [lax.rem(x + dx, 4) for dx in (2, 1, 3, 0)]

        @pl.loop(0, 8)
        def _(j):
            along = lax.rem(z + far_first(j), 8) * 2
            for plane in planes:
                for tx in groups:
                    if plane is planes[-1] and tx is groups[-1]:

                        @pl.when(j != 7)
                        def _():
                            pl.semaphore_signal(
                                barrier, inc=1, device_id=(plane + along, tx), device_id_type=MESH
                            )

                    else:
                        pl.semaphore_signal(barrier, inc=1, device_id=(plane + along, tx), device_id_type=MESH)

    for c in loads:
        c.wait()

    def mix(i, _):
        s = pl.ds(pl.multiple_of(i * STEP, STEP), STEP)
        g = g_buf[s]
        nm = momentum_decay * m_buf[s] + g
        nm_buf[s] = nm
        advance[s] = (g + momentum_decay * nm).astype(jnp.bfloat16)
        return 0

    lax.fori_loop(0, MATS // STEP, mix, 0)
    keep_momentum = pltpu.make_async_copy(nm_buf, new_momentum, store_sem.at[0])
    keep_momentum.start()

    own_count = jnp.where(owns, 1, 0)
    @pl.when(core == 0)
    def _():
        pl.semaphore_wait(barrier, MATS + 1 - own_count)
        pl.semaphore_signal(ready, inc=1, device_id=(dp + 1, x), device_id_type=MESH)

    @pl.when(core == 1)
    def _():
        pl.semaphore_wait(ready, 1)

    slot = z * 64 + y * 8 + core * 4 + x

    def send_to(count, first, turn):
        @pl.loop(0, count)
        def _(i):
            k = first + 2 * lax.rem(i + turn, count)
            six, d = offset_of(k)
            odd = jnp.where(six, 0, 1)
            for tx in range(4):
                ty = 1 - odd if tx % 2 else odd
                tz = lax.rem(ty + d + 2 * tx, 8)
                for pair in range(4):
                    there = ((2 * pair + ty) * 8 + tz) * 2
                    t = k * 16 + tx * 4 + pair

                    @pl.when(jnp.logical_or(there != dp, x != tx))
                    def _():
                        pltpu.make_async_remote_copy(
                            src_ref=advance.at[t], dst_ref=arrived.at[slot], send_sem=send_sem, recv_sem=recv_sem,
                            device_id=(there, tx), device_id_type=MESH,
                        ).start()

                    tz = tz + 2
                    tz = jnp.where(tz >= 8, tz - 8, tz)

    send_to(6, 0, z)
    send_to(5, 1, z)

    @pl.when(owns)
    def _():
        own = pltpu.make_async_copy(advance.at[mine], arrived.at[slot], own_sem.at[0])
        own.start()
        own.wait()
        pltpu.make_async_copy(
            arrived.at[pl.ds(0, DEVICES - 1)], arrived.at[pl.ds(0, DEVICES - 1)], recv_sem
        ).wait()

        def gather(i, _):
            block = arrived[pl.ds(pl.multiple_of(i * 32, 32), 32)].reshape(64, COLS)
            current[pl.ds(pl.multiple_of(i * 64, 64), 64), :] = block
            return 0

        lax.fori_loop(0, DEVICES // 32, gather, 0)
        scale = make_gram(current, gram, True)
        make_poly(gram, poly)
        for i in range(ROWS // TILE):
            r = slice(i * TILE, (i + 1) * TILE)
            product = jnp.dot(current[r, :], poly[...], preferred_element_type=jnp.float32)
            after[r, :] = (scale * (coef_first * current[r, :].astype(jnp.float32) + product)).astype(jnp.bfloat16)
        make_gram(after, gram, False)
        make_poly(gram, poly)
        factor = rms_match * math.sqrt(max(ROWS, COLS))

        groups = [lax.rem(x + dx, 4) for dx in (2, 1, 3, 0)]

        def finish(i, _):
            plane = lax.div(i, 4) * 4 + lax.rem(z + i, 4)
            r = pl.ds(pl.multiple_of(plane * 128, 128), 128)
            rows = after[r, :]
            product = jnp.dot(rows, poly[...], preferred_element_type=jnp.float32)
            rows = (coef_first * rows.astype(jnp.float32) + product).astype(jnp.bfloat16)
            rows = (factor * rows.astype(jnp.float32)).astype(jnp.bfloat16)
            finished[pl.ds(pl.multiple_of(plane * 64, 64), 64)] = rows.reshape(64, 2, COLS)

            @pl.loop(0, 8)
            def _(j):
                ty = lax.div(j, 4) * 4 + lax.rem(y + j, 4)
                there = (ty * 8 + plane) * 2
                row = plane * 64 + ty * 8
                for way in range(8):
                    tx = groups[way % 4]
                    td = there + way // 4

                    @pl.when(jnp.logical_or(td != dp, tx != x))
                    def _():
                        pltpu.make_async_remote_copy(
                            src_ref=finished.at[row + way // 4 * 4 + tx], dst_ref=returned.at[mine],
                            send_sem=back_send, recv_sem=back_recv, device_id=(td, tx), device_id_type=MESH,
                        ).start()

            return 0

        lax.fori_loop(0, 8, finish, 0)
        own_back = pltpu.make_async_copy(finished.at[slot], returned.at[mine], own_sem.at[1])
        own_back.start()
        own_back.wait()
        pltpu.make_async_copy(
            advance.at[pl.ds(0, MATS - 1)], advance.at[pl.ds(0, MATS - 1)], send_sem
        ).wait()
        pltpu.make_async_copy(
            returned.at[pl.ds(0, MATS - 1)], returned.at[pl.ds(0, MATS - 1)], back_recv
        ).wait()
        pltpu.make_async_copy(
            finished.at[pl.ds(0, DEVICES - 1)], finished.at[pl.ds(0, DEVICES - 1)], back_send
        ).wait()

    @pl.when(jnp.logical_not(owns))
    def _():
        pltpu.make_async_copy(advance, advance, send_sem).wait()
        pltpu.make_async_copy(returned, returned, back_recv).wait()

    keep_momentum.wait()


def last_step(new_momentum_in, update_in, weight, new_momentum, update, new_weight, u_buf, w_buf, nw_buf, nm_buf, part_sem):
    size = MATS // PARTS
    parts = [pl.ds(i * size, size) for i in range(PARTS)]
    loads = [
        (
            pltpu.make_async_copy(update_in.at[p], u_buf.at[p], part_sem.at[0, i]),
            pltpu.make_async_copy(weight.at[p], w_buf.at[p], part_sem.at[1, i]),
        )
        for i, p in enumerate(parts)
    ]
    for pair in loads:
        for c in pair:
            c.start()
    keeps = [pltpu.make_async_copy(new_momentum_in.at[p], nm_buf.at[p], part_sem.at[4, i]) for i, p in enumerate(parts)]
    for c in keeps:
        c.start()
    stores = []
    for i, p in enumerate(parts):
        for c in loads[i]:
            c.wait()
        stores.append(pltpu.make_async_copy(u_buf.at[p], update.at[p], part_sem.at[2, i]))
        stores[-1].start()

        def step(j, _):
            s = pl.ds(pl.multiple_of(i * size + j * (size // 2), size // 2), size // 2)
            nw_buf[s] = (
                (1.0 - learning_rate * weight_decay) * w_buf[s].astype(jnp.float32)
                - learning_rate * u_buf[s].astype(jnp.float32)
            ).astype(jnp.bfloat16)
            return 0

        lax.fori_loop(0, 2, step, 0)
        stores.append(pltpu.make_async_copy(nw_buf.at[p], new_weight.at[p], part_sem.at[3, i]))
        stores[-1].start()
        keeps[i].wait()
        stores.append(pltpu.make_async_copy(nm_buf.at[p], new_momentum.at[p], part_sem.at[5, i]))
        stores[-1].start()
    for c in stores:
        c.wait()


def per_device(gradient, momentum, weight):
    shape = gradient.shape
    f32, bf16 = jnp.float32, jnp.bfloat16
    blocks = (DEVICES,) + shape[1:]
    new_momentum, update = pl.pallas_call(
        kernel,
        out_shape=(jax.ShapeDtypeStruct(shape, f32), jax.ShapeDtypeStruct(shape, bf16)),
        in_specs=[pl.BlockSpec(memory_space=pl.ANY)] * 2,
        out_specs=[pl.BlockSpec(memory_space=pl.ANY)] * 2,
        scratch_shapes=[
            pltpu.VMEM(shape, f32),
            pltpu.VMEM(shape, f32),
            pltpu.VMEM(shape, f32),
            pltpu.VMEM(shape, bf16),
            pltpu.VMEM(blocks, bf16),
            pltpu.VMEM((ROWS, COLS), bf16),
            pltpu.VMEM((ROWS, COLS), bf16),
            pltpu.VMEM((COLS, COLS), bf16),
            pltpu.VMEM((COLS, COLS), bf16),
            pltpu.VMEM(blocks, bf16),
            pltpu.SemaphoreType.REGULAR,
            pltpu.SemaphoreType.DMA((2,)),
            pltpu.SemaphoreType.DMA((1,)),
            pltpu.SemaphoreType.DMA((2,)),
            pltpu.SemaphoreType.DMA,
            pltpu.SemaphoreType.DMA,
            pltpu.SemaphoreType.DMA,
            pltpu.SemaphoreType.DMA,
        ],
        compiler_params=pltpu.CompilerParams(
            collective_id=0, has_side_effects=True, vmem_limit_bytes=60 * 2**20
        ),
    )(gradient, momentum)
    return pl.pallas_call(
        last_step,
        out_shape=(
            jax.ShapeDtypeStruct(shape, f32),
            jax.ShapeDtypeStruct(shape, bf16),
            jax.ShapeDtypeStruct(shape, bf16),
        ),
        in_specs=[pl.BlockSpec(memory_space=pl.ANY)] * 3,
        out_specs=[pl.BlockSpec(memory_space=pl.ANY)] * 3,
        scratch_shapes=[pltpu.VMEM(shape, bf16)] * 3
        + [pltpu.VMEM(shape, f32), pltpu.SemaphoreType.DMA((6, PARTS))],
        compiler_params=pltpu.CompilerParams(vmem_limit_bytes=60 * 2**20),
    )(new_momentum, update, weight)


def solution(mesh):
    spec = P(None, ("dp", "group"), None)
    return jax.shard_map(
        per_device, mesh=mesh, in_specs=(spec, spec, spec), out_specs=(spec, spec, spec), check_vma=False
    )
```

```python
import math

import jax
import jax.numpy as jnp
from jax import lax
from jax.experimental import pallas as pl
from jax.experimental.pallas import tpu as pltpu
from jax.sharding import PartitionSpec as P

ROWS = 1024
COLS = 768
ITERS = 2
MATS = 176
DEVICES = 512

momentum_decay = 0.95
coef_first = 3.4445
coef_second = -4.775
coef_third = 2.0315
epsilon_norm = 1e-07
learning_rate = 0.02
weight_decay = 0.1
rms_match = 0.2

MESH = pl.DeviceIdType.MESH
TILE = 256
STEP = 16
PARTS = 4
FAR = (4, 3, 5, 2, 6, 1, 7, 0)


def offset_of(k):
    six = k < 6
    kk = jnp.where(six, k, k - 6)
    last = jnp.logical_and(jnp.logical_not(six), kk >= 4)
    return six, kk + 1 + jnp.where(kk >= 2, 1, 0) + jnp.where(last, 1, 0)


def owner_of(q, six, d):
    x = lax.div(q, 4)
    parity = lax.rem(x, 2)
    y = 2 * lax.rem(q, 4) + jnp.where(six, parity, 1 - parity)
    z = lax.rem(y + d + 2 * x, 8)
    return (y * 8 + z) * 2, x


def matrix_of(dp, x):
    core = lax.rem(dp, 2)
    place = lax.div(dp, 2)
    y = lax.div(place, 8)
    z = lax.rem(place, 8)
    d = lax.rem(z - y - 2 * x + 16, 8)
    six = lax.rem(y, 2) == lax.rem(x, 2)
    gap = jnp.logical_or(d == 0, d == 3)
    gap = jnp.logical_or(gap, jnp.logical_and(jnp.logical_not(six), d == 6))
    owns = jnp.logical_and(core == 0, jnp.logical_not(gap))
    kk = d - 1 - jnp.where(d >= 4, 1, 0)
    kk = kk - jnp.where(jnp.logical_and(jnp.logical_not(six), d >= 7), 1, 0)
    k = jnp.where(six, kk, kk + 6)
    t = k * 16 + x * 4 + lax.div(y, 2)
    return owns, jnp.where(owns, t, 0)


def far_first(a):
    half = lax.div(a, 2)
    return jnp.where(lax.rem(a, 2) == 0, 4 - half, lax.rem(5 + half, 8))


def dot_first(a, b):
    return lax.dot_general(a, b, (((0,), (0,)), ((), ())), preferred_element_type=jnp.float32)


def make_gram(source, gram, norm):
    scale = None
    blocks = []
    for i in range(COLS // TILE):
        a = i * TILE
        blocks.append(dot_first(source[:, a : a + TILE], source[:, a:]))
    if norm:
        row = lax.broadcasted_iota(jnp.int32, (TILE, TILE), 0)
        column = lax.broadcasted_iota(jnp.int32, (TILE, TILE), 1)
        trace = jnp.zeros((1, 1), jnp.float32)
        for block in blocks:
            diagonal = jnp.where(row == column, block[:, :TILE], 0.0)
            trace = trace + jnp.sum(diagonal, axis=(0, 1), keepdims=True)
        scale = 1.0 / (jnp.sqrt(trace) + epsilon_norm)
        blocks = [(block * scale) * scale for block in blocks]
    for i, block in enumerate(blocks):
        a = i * TILE
        block = block.astype(jnp.bfloat16)
        gram[a : a + TILE, a:] = block
        for j in range(i + 1, COLS // TILE):
            gram[j * TILE : (j + 1) * TILE, a : a + TILE] = block[:, (j - i) * TILE : (j - i + 1) * TILE].T
    return scale


def make_poly(gram, poly):
    for i in range(COLS // TILE):
        a = i * TILE
        squared = jnp.dot(gram[a : a + TILE, :], gram[:, a:], preferred_element_type=jnp.float32)
        block = (coef_second * gram[a : a + TILE, a:].astype(jnp.float32) + coef_third * squared).astype(jnp.bfloat16)
        poly[a : a + TILE, a:] = block
        for j in range(i + 1, COLS // TILE):
            poly[j * TILE : (j + 1) * TILE, a : a + TILE] = block[:, (j - i) * TILE : (j - i + 1) * TILE].T


def kernel(
    gradient, momentum,
    new_momentum, returned,
    g_buf, m_buf, nm_buf, advance, arrived, current, after, gram, poly, finished,
    ready, load_sem, store_sem, own_sem, send_sem, recv_sem, back_send, back_recv,
):
    dp = lax.axis_index("dp")
    x = lax.axis_index("group")
    me = dp * 4 + x
    owns, mine = matrix_of(dp, x)
    barrier = pltpu.get_barrier_semaphore()

    place = lax.div(dp, 2)
    core = lax.rem(dp, 2)
    y, z = lax.div(place, 8), lax.rem(place, 8)

    loads = [
        pltpu.make_async_copy(gradient, g_buf, load_sem.at[0]),
        pltpu.make_async_copy(momentum, m_buf, load_sem.at[1]),
    ]
    for c in loads:
        c.start()
    @pl.when(core == 1)
    def _():
        pl.semaphore_signal(barrier, inc=1, device_id=(dp - 1, x), device_id_type=MESH)

    @pl.when(owns)
    def _():
        planes = [lax.rem(y + dy, 8) * 16 for dy in FAR]
        groups = [lax.rem(x + dx, 4) for dx in (2, 1, 3, 0)]

        @pl.loop(0, 8)
        def _(j):
            along = lax.rem(z + far_first(7 - j), 8) * 2
            for plane in planes:
                for tx in groups:
                    if plane is planes[-1] and tx is groups[-1]:

                        @pl.when(j != 0)
                        def _():
                            pl.semaphore_signal(
                                barrier, inc=1, device_id=(plane + along, tx), device_id_type=MESH
                            )

                    else:
                        pl.semaphore_signal(barrier, inc=1, device_id=(plane + along, tx), device_id_type=MESH)

    for c in loads:
        c.wait()

    def mix(i, _):
        s = pl.ds(pl.multiple_of(i * STEP, STEP), STEP)
        g = g_buf[s]
        nm = momentum_decay * m_buf[s] + g
        nm_buf[s] = nm
        advance[s] = (g + momentum_decay * nm).astype(jnp.bfloat16)
        return 0

    lax.fori_loop(0, MATS // STEP, mix, 0)
    keep_momentum = pltpu.make_async_copy(nm_buf, new_momentum, store_sem.at[0])
    keep_momentum.start()

    own_count = jnp.where(owns, 1, 0)
    @pl.when(core == 0)
    def _():
        pl.semaphore_wait(barrier, MATS + 1 - own_count)
        pl.semaphore_signal(ready, inc=1, device_id=(dp + 1, x), device_id_type=MESH)

    @pl.when(core == 1)
    def _():
        pl.semaphore_wait(ready, 1)

    slot = z * 64 + y * 8 + core * 4 + x

    def send_to(count, first, turn):
        @pl.loop(0, count)
        def _(i):
            k = first + 2 * lax.rem(i + turn, count)
            six, d = offset_of(k)
            odd = jnp.where(six, 0, 1)
            for tx in range(4):
                ty = 1 - odd if tx % 2 else odd
                tz = lax.rem(ty + d + 2 * tx, 8)
                for pair in range(4):
                    there = ((2 * pair + ty) * 8 + tz) * 2
                    t = k * 16 + tx * 4 + pair

                    @pl.when(jnp.logical_or(there != dp, x != tx))
                    def _():
                        pltpu.make_async_remote_copy(
                            src_ref=advance.at[t], dst_ref=arrived.at[slot], send_sem=send_sem, recv_sem=recv_sem,
                            device_id=(there, tx), device_id_type=MESH,
                        ).start()

                    tz = tz + 2
                    tz = jnp.where(tz >= 8, tz - 8, tz)

    send_to(6, 0, z)
    send_to(5, 1, z)

    @pl.when(owns)
    def _():
        own = pltpu.make_async_copy(advance.at[mine], arrived.at[slot], own_sem.at[0])
        own.start()
        own.wait()
        pltpu.make_async_copy(
            arrived.at[pl.ds(0, DEVICES - 1)], arrived.at[pl.ds(0, DEVICES - 1)], recv_sem
        ).wait()

        def gather(i, _):
            block = arrived[pl.ds(pl.multiple_of(i * 32, 32), 32)].reshape(64, COLS)
            current[pl.ds(pl.multiple_of(i * 64, 64), 64), :] = block
            return 0

        lax.fori_loop(0, DEVICES // 32, gather, 0)
        scale = make_gram(current, gram, True)
        make_poly(gram, poly)
        for i in range(ROWS // TILE):
            r = slice(i * TILE, (i + 1) * TILE)
            product = jnp.dot(current[r, :], poly[...], preferred_element_type=jnp.float32)
            after[r, :] = (scale * (coef_first * current[r, :].astype(jnp.float32) + product)).astype(jnp.bfloat16)
        make_gram(after, gram, False)
        make_poly(gram, poly)
        factor = rms_match * math.sqrt(max(ROWS, COLS))

        groups = [lax.rem(x + dx, 4) for dx in (2, 1, 3, 0)]

        def finish(i, _):
            plane = lax.div(i, 4) * 4 + lax.rem(z + i, 4)
            r = pl.ds(pl.multiple_of(plane * 128, 128), 128)
            rows = after[r, :]
            product = jnp.dot(rows, poly[...], preferred_element_type=jnp.float32)
            rows = (coef_first * rows.astype(jnp.float32) + product).astype(jnp.bfloat16)
            rows = (factor * rows.astype(jnp.float32)).astype(jnp.bfloat16)
            finished[pl.ds(pl.multiple_of(plane * 64, 64), 64)] = rows.reshape(64, 2, COLS)

            @pl.loop(0, 8)
            def _(j):
                ty = lax.div(j, 4) * 4 + lax.rem(y + j, 4)
                there = (ty * 8 + plane) * 2
                row = plane * 64 + ty * 8
                for way in range(8):
                    tx = groups[way % 4]
                    td = there + way // 4

                    @pl.when(jnp.logical_or(td != dp, tx != x))
                    def _():
                        pltpu.make_async_remote_copy(
                            src_ref=finished.at[row + way // 4 * 4 + tx], dst_ref=returned.at[mine],
                            send_sem=back_send, recv_sem=back_recv, device_id=(td, tx), device_id_type=MESH,
                        ).start()

            return 0

        lax.fori_loop(0, 8, finish, 0)
        own_back = pltpu.make_async_copy(finished.at[slot], returned.at[mine], own_sem.at[1])
        own_back.start()
        own_back.wait()
        pltpu.make_async_copy(
            advance.at[pl.ds(0, MATS - 1)], advance.at[pl.ds(0, MATS - 1)], send_sem
        ).wait()
        pltpu.make_async_copy(
            returned.at[pl.ds(0, MATS - 1)], returned.at[pl.ds(0, MATS - 1)], back_recv
        ).wait()
        pltpu.make_async_copy(
            finished.at[pl.ds(0, DEVICES - 1)], finished.at[pl.ds(0, DEVICES - 1)], back_send
        ).wait()

    @pl.when(jnp.logical_not(owns))
    def _():
        pltpu.make_async_copy(advance, advance, send_sem).wait()
        pltpu.make_async_copy(returned, returned, back_recv).wait()

    keep_momentum.wait()


def last_step(new_momentum_in, update_in, weight, new_momentum, update, new_weight, u_buf, w_buf, nw_buf, nm_buf, part_sem):
    size = MATS // PARTS
    parts = [pl.ds(i * size, size) for i in range(PARTS)]
    loads = [
        (
            pltpu.make_async_copy(update_in.at[p], u_buf.at[p], part_sem.at[0, i]),
            pltpu.make_async_copy(weight.at[p], w_buf.at[p], part_sem.at[1, i]),
        )
        for i, p in enumerate(parts)
    ]
    for pair in loads:
        for c in pair:
            c.start()
    keeps = [pltpu.make_async_copy(new_momentum_in.at[p], nm_buf.at[p], part_sem.at[4, i]) for i, p in enumerate(parts)]
    for c in keeps:
        c.start()
    stores = []
    for i, p in enumerate(parts):
        for c in loads[i]:
            c.wait()
        stores.append(pltpu.make_async_copy(u_buf.at[p], update.at[p], part_sem.at[2, i]))
        stores[-1].start()

        def step(j, _):
            s = pl.ds(pl.multiple_of(i * size + j * (size // 2), size // 2), size // 2)
            nw_buf[s] = (
                (1.0 - learning_rate * weight_decay) * w_buf[s].astype(jnp.float32)
                - learning_rate * u_buf[s].astype(jnp.float32)
            ).astype(jnp.bfloat16)
            return 0

        lax.fori_loop(0, 2, step, 0)
        stores.append(pltpu.make_async_copy(nw_buf.at[p], new_weight.at[p], part_sem.at[3, i]))
        stores[-1].start()
        keeps[i].wait()
        stores.append(pltpu.make_async_copy(nm_buf.at[p], new_momentum.at[p], part_sem.at[5, i]))
        stores[-1].start()
    for c in stores:
        c.wait()


def per_device(gradient, momentum, weight):
    shape = gradient.shape
    f32, bf16 = jnp.float32, jnp.bfloat16
    blocks = (DEVICES,) + shape[1:]
    new_momentum, update = pl.pallas_call(
        kernel,
        out_shape=(jax.ShapeDtypeStruct(shape, f32), jax.ShapeDtypeStruct(shape, bf16)),
        in_specs=[pl.BlockSpec(memory_space=pl.ANY)] * 2,
        out_specs=[pl.BlockSpec(memory_space=pl.ANY)] * 2,
        scratch_shapes=[
            pltpu.VMEM(shape, f32),
            pltpu.VMEM(shape, f32),
            pltpu.VMEM(shape, f32),
            pltpu.VMEM(shape, bf16),
            pltpu.VMEM(blocks, bf16),
            pltpu.VMEM((ROWS, COLS), bf16),
            pltpu.VMEM((ROWS, COLS), bf16),
            pltpu.VMEM((COLS, COLS), bf16),
            pltpu.VMEM((COLS, COLS), bf16),
            pltpu.VMEM(blocks, bf16),
            pltpu.SemaphoreType.REGULAR,
            pltpu.SemaphoreType.DMA((2,)),
            pltpu.SemaphoreType.DMA((1,)),
            pltpu.SemaphoreType.DMA((2,)),
            pltpu.SemaphoreType.DMA,
            pltpu.SemaphoreType.DMA,
            pltpu.SemaphoreType.DMA,
            pltpu.SemaphoreType.DMA,
        ],
        compiler_params=pltpu.CompilerParams(
            collective_id=0, has_side_effects=True, vmem_limit_bytes=60 * 2**20
        ),
    )(gradient, momentum)
    return pl.pallas_call(
        last_step,
        out_shape=(
            jax.ShapeDtypeStruct(shape, f32),
            jax.ShapeDtypeStruct(shape, bf16),
            jax.ShapeDtypeStruct(shape, bf16),
        ),
        in_specs=[pl.BlockSpec(memory_space=pl.ANY)] * 3,
        out_specs=[pl.BlockSpec(memory_space=pl.ANY)] * 3,
        scratch_shapes=[pltpu.VMEM(shape, bf16)] * 3
        + [pltpu.VMEM(shape, f32), pltpu.SemaphoreType.DMA((6, PARTS))],
        compiler_params=pltpu.CompilerParams(vmem_limit_bytes=60 * 2**20),
    )(new_momentum, update, weight)


def solution(mesh):
    spec = P(None, ("dp", "group"), None)
    return jax.shard_map(
        per_device, mesh=mesh, in_specs=(spec, spec, spec), out_specs=(spec, spec, spec), check_vma=False
    )
```
